32 devices in a mesh: gx: 4 (over y, core), gy: 4 (over z), gz: 2 (over x).
Axes of the slice: x: 2, y: 2, z: 4, core: 2. Of those that a mesh axis runs over, the one named last changes fastest.
Arguments:
- hidden_states: bfloat16 [2048, 8192], P(None, ('gx', 'gz')), may hold values from -9.5 to 9.5
- grad_out: bfloat16 [2048, 8192], P(None, ('gx', 'gz')), may hold values from -6 to 6
- query_weight: bfloat16 [8192, 8192], P(('gx', 'gz'), 'gy'), may hold values from -0.0625 to 0.0625
- key_weight: bfloat16 [8192, 1024], P(('gx', 'gz'), 'gy'), may hold values from -0.0625 to 0.0625
- value_weight: bfloat16 [8192, 1024], P(('gx', 'gz'), 'gy'), may hold values from -0.0625 to 0.0625
- output_weight: bfloat16 [8192, 8192], P('gy', ('gx', 'gz')), may hold values from -0.0625 to 0.0625
- segment_ids: int32 [2048], P('gz'), may hold values from 0 to 3, as said below
- positions: int32 [2048], P('gz'), may hold values from 0 to 767, as said below
Outputs:
- input_grad: bfloat16 [2048, 8192], P('gy', ('gx', 'gz'))
- query_weight_grad: bfloat16 [8192, 8192], P(('gx', 'gz'), 'gy')
- key_weight_grad: bfloat16 [8192, 1024], P(('gx', 'gz'), 'gy')
- value_weight_grad: bfloat16 [8192, 1024], P(('gx', 'gz'), 'gy')
- output_weight_grad: bfloat16 [8192, 8192], P('gy', ('gx', 'gz'))
The draws below stay inside these ranges and needn't reach their ends.
Inputs may be any that keep to these rules, and one draw needn't show every extreme that they name: `segment_ids`: tokens come in aligned blocks of 1024; block b holds a chosen sequence with id 2 b followed by its rejected sequence with id 2 b + 1, each of 256 tokens or more. Within each sequence the positions run 0, 1, 2, ... in token order.
All inputs are finite; a program needn't handle non-finite values.
Results may differ from the reference program's by a relative error of at most 0.03.
Values may be sent and summed in bfloat16 or wider, within the bound.
A program may use at most 192 MiB of HBM per device.

```python
import math
import jax
import jax.numpy as jnp
from jax import lax

D = 8192
HQ = 64
KVH = 8
HD = 128
TZ = 1024
TOKENS = 2048
N_GX = 4
N_GY = 4
N_GZ = 2


def chosen_lengths(key):
    block_count = TOKENS // TZ
    offsets = jax.random.randint(jax.random.fold_in(key, 17), (block_count,), -(TZ // 4), TZ // 4 + 1)
    offsets = offsets.at[0].set(TZ // 4)
    return TZ // 2 + offsets


def draw_segment_ids(key, part):
    lengths = chosen_lengths(key)
    within = jnp.arange(TZ, dtype=jnp.int32)
    rejected = (within[None, :] >= lengths[:, None]).astype(jnp.int32)
    block_count = TOKENS // TZ
    numbers = 2 * jnp.arange(block_count, dtype=jnp.int32)[:, None] + rejected
    return numbers.reshape(TOKENS)


def draw_positions(key, part):
    lengths = chosen_lengths(key)
    within = jnp.arange(TZ, dtype=jnp.int32)[None, :]
    places = jnp.where(within < lengths[:, None], within, within - lengths[:, None])
    return places.reshape(TOKENS).astype(jnp.int32)


def draw_hidden_states(key, part):
    key = jax.random.fold_in(key, 3)
    base_key = jax.random.fold_in(key, 0)
    return jnp.clip(jax.random.normal(base_key, (TOKENS, D), jnp.float32), -6.0, 6.0).astype(jnp.bfloat16)


def block_scale(stream_key, extent, shards, smallest, high):
    factor_of, own = 1.0, jax.random.fold_in(stream_key, 6)
    for dim, blocks in shards:
        heights = jnp.exp(jax.random.uniform(jax.random.fold_in(own, dim), (blocks,), jnp.float32, smallest / len(shards), high / len(shards)))
        factor_of = factor_of * jnp.repeat(heights, extent[dim] // blocks).reshape([-1 if axis == dim else 1 for axis in range(len(extent))])
    return factor_of


def centred(rng, dims, width, bound, cuts=(), kind=jnp.bfloat16):
    result = jax.random.normal(rng, dims, jnp.float32) * width
    if len(cuts) > 0:
        result = block_scale(rng, dims, cuts, -0.22, 0.18) * result
    return jnp.clip(result, min=-bound, max=bound).astype(kind)


def setup_inputs(seed: int = 0) -> dict:
    arg_keys = jax.random.split(jax.random.key(seed), 9)
    return {
        "hidden_states": draw_hidden_states(jax.random.fold_in(arg_keys[8], 71), 0),
        "grad_out": centred(arg_keys[1], (TOKENS, D), 1.0, 6.0, ((1, 8),)),
        "query_weight": centred(arg_keys[2], (D, HQ * HD), D ** -0.5, 0.0625, ((0, 8), (1, 4))),
        "key_weight": centred(arg_keys[3], (D, KVH * HD), D ** -0.5, 0.0625, ((0, 8), (1, 4))),
        "value_weight": centred(arg_keys[4], (D, KVH * HD), D ** -0.5, 0.0625, ((0, 8), (1, 4))),
        "output_weight": centred(arg_keys[5], (HQ * HD, D), (HQ * HD) ** -0.5, 0.0625, ((0, 4), (1, 8))),
        "segment_ids": draw_segment_ids(jax.random.fold_in(arg_keys[8], 71), 0),
        "positions": draw_positions(jax.random.fold_in(arg_keys[8], 71), 0),
    }


rope_base = 10000.0
masked_score = -1e+30

def rope_tables(positions):
    halves = jnp.arange(HD // 2, dtype=jnp.float32)
    inverse = rope_base ** (-2.0 * halves / HD)
    angles = positions.astype(jnp.float32)[:, None] * inverse[None, :]
    return (jnp.cos(angles), jnp.sin(angles))

def rotate(values, cosine, sine, direction):
    middle = values.shape[-1] // 2
    leading = values[..., :middle]
    trailing = values[..., middle:]
    cosine_b = cosine[:, None, :]
    sine_b = sine[:, None, :] * direction
    return jnp.concatenate([leading * cosine_b - trailing * sine_b, trailing * cosine_b + leading * sine_b], axis=-1)

def piece_sum(left, right, pieces):
    breadth = left.shape[1] // pieces

    def add_piece(piece_index, running):
        offset = (piece_index * breadth).astype(jnp.int32)
        left_piece = lax.dynamic_slice_in_dim(left, offset, breadth, 1)
        right_piece = lax.dynamic_slice_in_dim(right, offset, breadth, 0)
        partial_term = jnp.dot(left_piece, right_piece, preferred_element_type=jnp.float32)
        rounded = lax.optimization_barrier(partial_term.astype(jnp.bfloat16))
        return running + rounded.astype(jnp.float32)
    initial = jnp.zeros((left.shape[0], right.shape[1]), jnp.float32)
    return lax.fori_loop(0, pieces, add_piece, initial)

def attend(query_in, key_in, value_in, grad_in, allowed):
    scale = 1.0 / math.sqrt(HD)
    query_f = query_in.astype(jnp.float32)
    key_f = key_in.astype(jnp.float32)
    value_f = value_in.astype(jnp.float32)
    grad_f = grad_in.astype(jnp.float32)
    scores = jnp.einsum('zqd,zkd->zqk', query_f, key_f) * scale
    scores = jnp.where(allowed, scores, masked_score)
    largest = lax.optimization_barrier(jnp.max(scores, axis=-1, keepdims=True))
    weights = jnp.exp(scores - largest)
    probs = weights / lax.optimization_barrier(jnp.sum(weights, axis=-1, keepdims=True))
    probs_low = probs.astype(jnp.bfloat16).astype(jnp.float32)
    outputs = jnp.einsum('zqk,zkd->zqd', probs_low, value_f).astype(jnp.bfloat16)
    delta = lax.optimization_barrier(jnp.sum(grad_f * outputs.astype(jnp.float32), axis=-1, keepdims=True))
    dprob = jnp.einsum('zqd,zkd->zqk', grad_f, value_f)
    dscore = (probs * (dprob - delta)).astype(jnp.bfloat16).astype(jnp.float32)
    dquery = jnp.einsum('zqk,zkd->zqd', dscore, key_f) * scale
    dkey = jnp.einsum('zqk,zqd->zkd', dscore, query_f) * scale
    dvalue = jnp.einsum('zqk,zqd->zkd', probs_low, grad_f)
    return (outputs, dquery, dkey, dvalue)

def reference(hidden_states, grad_out, query_weight, key_weight, value_weight, output_weight, segment_ids, positions):
    pieces = N_GX * N_GZ
    blocks = TOKENS // TZ
    grouping = HQ // KVH
    query = piece_sum(hidden_states, query_weight, pieces)
    keys = piece_sum(hidden_states, key_weight, pieces)
    values = piece_sum(hidden_states, value_weight, pieces)
    grad_heads = piece_sum(grad_out, output_weight.T, pieces)
    cosine, sine = rope_tables(positions)
    query_rot = rotate(query.reshape(TOKENS, HQ, HD), cosine, sine, 1.0).astype(jnp.bfloat16)
    key_rot = rotate(keys.reshape(TOKENS, KVH, HD), cosine, sine, 1.0).astype(jnp.bfloat16)
    value_low = values.reshape(TOKENS, KVH, HD).astype(jnp.bfloat16)
    grad_low = grad_heads.reshape(TOKENS, HQ, HD).astype(jnp.bfloat16)
    segment_blocks = segment_ids.reshape(blocks, TZ)
    position_blocks = positions.reshape(blocks, TZ)
    allowed = (segment_blocks[:, :, None] == segment_blocks[:, None, :]) & (position_blocks[:, None, :] <= position_blocks[:, :, None])
    query_heads = query_rot.reshape(blocks, TZ, HQ, HD)
    key_heads = key_rot.reshape(blocks, TZ, KVH, HD)
    value_heads = value_low.reshape(blocks, TZ, KVH, HD)
    grad_heads4 = grad_low.reshape(blocks, TZ, HQ, HD)

    def one_head(head_index):
        shared_head = head_index // grouping
        query_one = lax.dynamic_index_in_dim(query_heads, head_index, 2, False)
        key_one = lax.dynamic_index_in_dim(key_heads, shared_head, 2, False)
        value_one = lax.dynamic_index_in_dim(value_heads, shared_head, 2, False)
        grad_one = lax.dynamic_index_in_dim(grad_heads4, head_index, 2, False)
        return attend(query_one, key_one, value_one, grad_one, allowed)
    outputs, dquery, dkey, dvalue = lax.map(one_head, jnp.arange(HQ, dtype=jnp.int32))

    def flatten(stacked):
        return stacked.transpose(1, 2, 0, 3).reshape(TOKENS, HQ, HD)
    head_outputs = flatten(outputs).reshape(TOKENS, HQ * HD)
    dquery_low = rotate(flatten(dquery), cosine, sine, -1.0).astype(jnp.bfloat16)
    dkey_each = rotate(flatten(dkey), cosine, sine, -1.0).astype(jnp.bfloat16)
    dvalue_each = flatten(dvalue).astype(jnp.bfloat16)
    dkey_sum = dkey_each.astype(jnp.float32).reshape(TOKENS, KVH, grouping, HD).sum(axis=2).astype(jnp.bfloat16)
    dvalue_sum = dvalue_each.astype(jnp.float32).reshape(TOKENS, KVH, grouping, HD).sum(axis=2).astype(jnp.bfloat16)
    dquery_flat = dquery_low.reshape(TOKENS, HQ * HD)
    dkey_flat = dkey_sum.reshape(TOKENS, KVH * HD)
    dvalue_flat = dvalue_sum.reshape(TOKENS, KVH * HD)
    query_cols = HQ * HD // N_GY
    key_cols = KVH * HD // N_GY
    running = jnp.zeros((TOKENS, D), jnp.float32)
    for group_index in range(N_GY):
        query_part = dquery_flat[:, group_index * query_cols:(group_index + 1) * query_cols]
        key_part = dkey_flat[:, group_index * key_cols:(group_index + 1) * key_cols]
        value_part = dvalue_flat[:, group_index * key_cols:(group_index + 1) * key_cols]
        partial_term = jnp.dot(query_part, query_weight[:, group_index * query_cols:(group_index + 1) * query_cols].T, preferred_element_type=jnp.float32)
        partial_term = partial_term + jnp.dot(key_part, key_weight[:, group_index * key_cols:(group_index + 1) * key_cols].T, preferred_element_type=jnp.float32)
        partial_term = partial_term + jnp.dot(value_part, value_weight[:, group_index * key_cols:(group_index + 1) * key_cols].T, preferred_element_type=jnp.float32)
        rounded = lax.optimization_barrier(partial_term.astype(jnp.bfloat16))
        running = running + rounded.astype(jnp.float32)
    input_grad = running.astype(jnp.bfloat16)
    query_weight_grad = jnp.dot(hidden_states.T, dquery_flat, preferred_element_type=jnp.float32).astype(jnp.bfloat16)
    key_weight_grad = jnp.dot(hidden_states.T, dkey_flat, preferred_element_type=jnp.float32).astype(jnp.bfloat16)
    value_weight_grad = jnp.dot(hidden_states.T, dvalue_flat, preferred_element_type=jnp.float32).astype(jnp.bfloat16)
    output_weight_grad = jnp.dot(head_outputs.T, grad_out, preferred_element_type=jnp.float32).astype(jnp.bfloat16)
    return (input_grad, query_weight_grad, key_weight_grad, value_weight_grad, output_weight_grad)
```

```python
import functools
import math

import jax
import jax.numpy as jnp
from jax import lax
from jax.experimental import pallas as pl
from jax.experimental.pallas import tpu as pltpu
from jax.sharding import PartitionSpec as P

HD = 128
GROUP = ("gx", "gz")

rope_base = 10000.0
masked_score = -1e30
VMEM_LIMIT = 56 * 1024 * 1024


def params():
    return pltpu.CompilerParams(vmem_limit_bytes=VMEM_LIMIT)


def cost(flops, moved):
    return pl.CostEstimate(flops=flops, bytes_accessed=moved, transcendentals=0)


def dot(a, b, ca, cb):
    return lax.dot_general(a, b, (((ca,), (cb,)), ((), ())), preferred_element_type=jnp.float32)


def rope_tables(positions, head_size):
    halves = jnp.arange(head_size // 2, dtype=jnp.float32)
    inverse = rope_base ** (-2.0 * halves / head_size)
    angles = positions.astype(jnp.float32)[:, None] * inverse[None, :]
    cosine, sine = jnp.cos(angles), jnp.sin(angles)
    return jnp.concatenate([cosine, cosine], axis=1), jnp.concatenate([-sine, sine], axis=1)


def rotate(values, cosine, sine):
    return values * cosine + pltpu.roll(values, values.shape[-1] // 2, 1) * sine


def project_kernel(x_ref, w_ref, o_ref, *, contract):
    o_ref[...] = dot(x_ref[...], w_ref[...], 1, contract).astype(o_ref.dtype)


def project(x, weight, across, transposed):
    tokens, depth = x.shape
    columns = weight.shape[0 if transposed else 1] // across
    tile = min(512, tokens)
    steps = tokens // tile
    if transposed:
        w_spec = pl.BlockSpec((columns, depth), lambda m, t: (m, 0))
    else:
        w_spec = pl.BlockSpec((depth, columns), lambda m, t: (0, m))
    return pl.pallas_call(
        functools.partial(project_kernel, contract=1 if transposed else 0),
        grid=(across, steps),
        out_shape=jax.ShapeDtypeStruct((across * tokens, columns), jnp.bfloat16),
        in_specs=[pl.BlockSpec((tile, depth), lambda m, t: (t, 0)), w_spec],
        out_specs=pl.BlockSpec((tile, columns), lambda m, t: (m * steps + t, 0)),
        compiler_params=params(),
        cost_estimate=cost(2 * tokens * depth * columns * across, 16 * 2**20),
    )(x, weight)


def project_kv_kernel(x_ref, k_ref, v_ref, o_ref):
    x = x_ref[...]
    o_ref[:, :HD] = dot(x, k_ref[...], 1, 0).astype(o_ref.dtype)
    o_ref[:, HD:] = dot(x, v_ref[...], 1, 0).astype(o_ref.dtype)


def project_kv(x, key_weight, value_weight, sharers, depth_count):
    tokens, depth = x.shape
    kv_groups = key_weight.shape[1] // HD
    rows = tokens // depth_count // sharers
    w_spec = pl.BlockSpec((depth, HD), lambda g, s, z: (0, g))
    return pl.pallas_call(
        project_kv_kernel,
        grid=(kv_groups, sharers, depth_count),
        out_shape=jax.ShapeDtypeStruct((kv_groups * tokens, 2 * HD), jnp.bfloat16),
        in_specs=[
            pl.BlockSpec((rows, depth), lambda g, s, z: (z * sharers + s, 0)),
            w_spec,
            w_spec,
        ],
        out_specs=pl.BlockSpec(
            (rows, 2 * HD), lambda g, s, z: ((g * sharers + s) * depth_count + z, 0)
        ),
        compiler_params=params(),
        cost_estimate=cost(4 * tokens * depth * HD * kv_groups, 8 * 2**20),
    )(x, key_weight, value_weight)


def attend_kernel(
    q_ref, g_ref, kv_ref, cos_ref, sin_ref, seg_col, seg_row, o_ref, dq_ref, dkv_ref, dk_acc, dv_acc, kr_ref, *, tile
):
    head = pl.program_id(0)
    rows = q_ref.shape[0]
    scale = 1.0 / math.sqrt(HD)

    @pl.when(head == 0)
    def _():
        dk_acc[...] = jnp.zeros_like(dk_acc)
        dv_acc[...] = jnp.zeros_like(dv_acc)
        keys = kv_ref[:, :HD].astype(jnp.float32)
        kr_ref[...] = rotate(keys, cos_ref[...], sin_ref[...]).astype(kr_ref.dtype)

    for step in range(rows // tile):
        here = pl.ds(step * tile, tile)
        width = (step + 1) * tile
        cosine, sine = cos_ref[here, :], sin_ref[here, :]
        query = rotate(q_ref[here, :].astype(jnp.float32), cosine, sine).astype(jnp.bfloat16)
        grad = g_ref[here, :].astype(jnp.bfloat16)
        keys = kr_ref[:width, :]
        values = kv_ref[:width, HD:]
        scores = dot(query, keys, 1, 1) * scale
        at_row = lax.broadcasted_iota(jnp.int32, scores.shape, 0) + step * tile
        at_col = lax.broadcasted_iota(jnp.int32, scores.shape, 1)
        allowed = (seg_col[here, :] == seg_row[:, :width]) & (at_col <= at_row)
        scores = jnp.where(allowed, scores, masked_score)
        weights = jnp.exp(scores - jnp.max(scores, axis=-1, keepdims=True))
        probs = weights * (1.0 / jnp.sum(weights, axis=-1, keepdims=True))
        probs_low = probs.astype(jnp.bfloat16)
        outputs = dot(probs_low, values, 1, 0).astype(jnp.bfloat16)
        o_ref[here, :] = outputs
        delta = jnp.sum(
            grad.astype(jnp.float32) * outputs.astype(jnp.float32), axis=-1, keepdims=True
        )
        dscore = (probs * (dot(grad, values, 1, 1) - delta)).astype(jnp.bfloat16)
        dquery = dot(dscore, keys, 1, 0) * scale
        dq_ref[here, :] = rotate(dquery, cosine, -sine).astype(dq_ref.dtype)
        dk_acc[:width, :] += dot(dscore, query, 0, 0) * scale
        dv_acc[:width, :] += dot(probs_low, grad, 0, 0)

    @pl.when(head == pl.num_programs(0) - 1)
    def _():
        dkv_ref[:, :HD] = rotate(dk_acc[...], cos_ref[...], -sin_ref[...]).astype(dkv_ref.dtype)
        dkv_ref[:, HD:] = dv_acc[...].astype(dkv_ref.dtype)


def attend(query, grad, kv, cosine, sine, segments):
    rows, columns = query.shape
    heads = columns // HD
    head_spec = pl.BlockSpec((rows, HD), lambda h: (0, h))

    def whole(shape):
        return pl.BlockSpec(shape, lambda h: (0, 0))

    return pl.pallas_call(
        functools.partial(attend_kernel, tile=min(256, rows)),
        grid=(heads,),
        out_shape=(
            jax.ShapeDtypeStruct((rows, columns), jnp.bfloat16),
            jax.ShapeDtypeStruct((rows, columns), jnp.bfloat16),
            jax.ShapeDtypeStruct((rows, 2 * HD), jnp.bfloat16),
        ),
        in_specs=[
            head_spec,
            head_spec,
            whole((rows, 2 * HD)),
            whole((rows, HD)),
            whole((rows, HD)),
            whole((rows, 1)),
            whole((1, rows)),
        ],
        out_specs=(head_spec, head_spec, whole((rows, 2 * HD))),
        scratch_shapes=[
            pltpu.VMEM((rows, HD), jnp.float32),
            pltpu.VMEM((rows, HD), jnp.float32),
            pltpu.VMEM((rows, HD), jnp.bfloat16),
        ],
        compiler_params=params(),
        cost_estimate=cost(10 * rows * rows * columns, 8 * 2**20),
    )(query, grad, kv, cosine, sine, segments[:, None], segments[None, :])


def input_grad_kernel(dq_ref, dkv_ref, wq_ref, wk_ref, wv_ref, o_ref):
    across, _, columns = dq_ref.shape
    total = None
    for m in range(across):
        term = dot(dq_ref[m], wq_ref[:, m * columns : (m + 1) * columns], 1, 1)
        total = term if total is None else total + term
    for g in range(dkv_ref.shape[0]):
        both = dkv_ref[g]
        total = total + dot(both[:, :HD], wk_ref[:, g * HD : (g + 1) * HD], 1, 1)
        total = total + dot(both[:, HD:], wv_ref[:, g * HD : (g + 1) * HD], 1, 1)
    o_ref[...] = total.astype(o_ref.dtype)


def input_grad_part(dq, dkv, wq, wk, wv):
    across, tokens, columns = dq.shape
    groups = dkv.shape[0]
    breadth = wq.shape[0]
    tile = min(256, tokens)

    def whole(x):
        return pl.BlockSpec(x.shape, lambda t: (0, 0))

    return pl.pallas_call(
        input_grad_kernel,
        grid=(tokens // tile,),
        out_shape=jax.ShapeDtypeStruct((tokens, breadth), jnp.bfloat16),
        in_specs=[
            pl.BlockSpec((across, tile, columns), lambda t: (0, t, 0)),
            pl.BlockSpec((groups, tile, 2 * HD), lambda t: (0, t, 0)),
            whole(wq),
            whole(wk),
            whole(wv),
        ],
        out_specs=pl.BlockSpec((tile, breadth), lambda t: (t, 0)),
        compiler_params=params(),
        cost_estimate=cost(2 * tokens * breadth * (columns * across + 2 * HD * groups), 2**24),
    )(dq, dkv, wq, wk, wv)


def qkv_grad_kernel(x_ref, dq_ref, dkv_ref, q_out, k_out, v_out, xt_ref):
    m = pl.program_id(0)

    @pl.when(m == 0)
    def _():
        xt_ref[...] = x_ref[...].T
        for g in range(dkv_ref.shape[0]):
            both = dot(xt_ref[...], dkv_ref[g], 1, 0).astype(k_out.dtype)
            k_out[:, g * HD : (g + 1) * HD] = both[:, :HD]
            v_out[:, g * HD : (g + 1) * HD] = both[:, HD:]

    q_out[...] = dot(xt_ref[...], dq_ref[0], 1, 0).astype(q_out.dtype)


def qkv_grads(x, dq, dkv):
    across, tokens, columns = dq.shape
    groups = dkv.shape[0]
    breadth = x.shape[1]
    return pl.pallas_call(
        qkv_grad_kernel,
        grid=(across,),
        out_shape=(
            jax.ShapeDtypeStruct((breadth, across * columns), jnp.bfloat16),
            jax.ShapeDtypeStruct((breadth, groups * HD), jnp.bfloat16),
            jax.ShapeDtypeStruct((breadth, groups * HD), jnp.bfloat16),
        ),
        in_specs=[
            pl.BlockSpec(x.shape, lambda m: (0, 0)),
            pl.BlockSpec((1, tokens, columns), lambda m: (m, 0, 0)),
            pl.BlockSpec(dkv.shape, lambda m: (0, 0, 0)),
        ],
        out_specs=(
            pl.BlockSpec((breadth, columns), lambda m: (0, m)),
            pl.BlockSpec((breadth, groups * HD), lambda m: (0, 0)),
            pl.BlockSpec((breadth, groups * HD), lambda m: (0, 0)),
        ),
        scratch_shapes=[pltpu.VMEM((breadth, tokens), jnp.bfloat16)],
        compiler_params=params(),
        cost_estimate=cost(2 * tokens * breadth * (columns * across + 2 * HD * groups), 2**24),
    )(x, dq, dkv)


def out_grad_kernel(a_ref, g_ref, o_ref):
    o_ref[...] = dot(a_ref[0].T, g_ref[...], 1, 0).astype(o_ref.dtype)


def out_grad(outputs, grad_out):
    across, tokens, columns = outputs.shape
    breadth = grad_out.shape[1]
    return pl.pallas_call(
        out_grad_kernel,
        grid=(across,),
        out_shape=jax.ShapeDtypeStruct((across * columns, breadth), jnp.bfloat16),
        in_specs=[
            pl.BlockSpec((1, tokens, columns), lambda m: (m, 0, 0)),
            pl.BlockSpec(grad_out.shape, lambda m: (0, 0)),
        ],
        out_specs=pl.BlockSpec((columns, breadth), lambda m: (m, 0)),
        compiler_params=params(),
        cost_estimate=cost(2 * tokens * breadth * columns * across, 2**24),
    )(outputs, grad_out)


def scatter_sum(x):
    return lax.psum_scatter(x, GROUP, scatter_dimension=0, tiled=True)


def gather(x):
    return lax.all_gather(x, GROUP, axis=0, tiled=True)


def per_device(
    hidden_states,
    grad_out,
    query_weight,
    key_weight,
    value_weight,
    output_weight,
    segment_ids,
    positions,
):
    across = lax.axis_size("gx")
    depth_count = lax.axis_size("gz")
    token_count = hidden_states.shape[0]
    kv_groups = key_weight.shape[1] // HD
    sharers = across // kv_groups
    columns = query_weight.shape[1] // across

    kv_part = project_kv(hidden_states, key_weight, value_weight, sharers, depth_count)
    kv_piece = scatter_sum(kv_part)
    kv = lax.all_gather(
        kv_piece,
        "gx",
        axis=0,
        tiled=True,
        axis_index_groups=[
            [g * sharers + s for s in range(sharers)] for g in range(kv_groups)
        ],
    )
    query = scatter_sum(project(hidden_states, query_weight, across, False))
    grad_heads = scatter_sum(project(grad_out, output_weight, across, True))
    cosine, sine = rope_tables(positions, HD)
    outputs, dquery, dkv = attend(query, grad_heads, kv, cosine, sine, segment_ids)

    dkv_all = (
        gather(dkv)
        .reshape(kv_groups, sharers, token_count, 2 * HD)
        .astype(jnp.float32)
        .sum(axis=1)
        .astype(jnp.bfloat16)
    )
    dq_all = gather(dquery).reshape(across, token_count, columns)
    summed = input_grad_part(dq_all, dkv_all, query_weight, key_weight, value_weight)
    input_grad = lax.psum_scatter(summed, "gy", scatter_dimension=0, tiled=True)
    outputs_all = gather(outputs).reshape(across, token_count, columns)
    query_weight_grad, key_weight_grad, value_weight_grad = qkv_grads(
        hidden_states, dq_all, dkv_all
    )
    output_weight_grad = out_grad(outputs_all, grad_out)
    return (input_grad, query_weight_grad, key_weight_grad, value_weight_grad, output_weight_grad)


def solution(mesh):
    placed = (
        P(None, GROUP),
        P(None, GROUP),
        P(GROUP, "gy"),
        P(GROUP, "gy"),
        P(GROUP, "gy"),
        P("gy", GROUP),
        P("gz"),
        P("gz"),
    )
    return jax.shard_map(
        per_device,
        mesh=mesh,
        in_specs=placed,
        out_specs=(
            P("gy", GROUP),
            P(GROUP, "gy"),
            P(GROUP, "gy"),
            P(GROUP, "gy"),
            P("gy", GROUP),
        ),
        check_vma=False,
    )
```

```python
import functools
import math

import jax
import jax.numpy as jnp
from jax import lax
from jax.experimental import pallas as pl
from jax.experimental.pallas import tpu as pltpu
from jax.sharding import PartitionSpec as P

HD = 128
GROUP = ("gx", "gz")
MESH = pl.DeviceIdType.MESH

rope_base = 10000.0
masked_score = -1e30
VMEM_LIMIT = 56 * 1024 * 1024


def params():
    return pltpu.CompilerParams(vmem_limit_bytes=VMEM_LIMIT)


def cost(flops, moved):
    return pl.CostEstimate(flops=flops, bytes_accessed=moved, transcendentals=0)


def dot(a, b, ca, cb):
    return lax.dot_general(a, b, (((ca,), (cb,)), ((), ())), preferred_element_type=jnp.float32)


def rope_tables(positions, head_size):
    halves = jnp.arange(head_size // 2, dtype=jnp.float32)
    inverse = rope_base ** (-2.0 * halves / head_size)
    angles = positions.astype(jnp.float32)[:, None] * inverse[None, :]
    cosine, sine = jnp.cos(angles), jnp.sin(angles)
    return jnp.concatenate([cosine, cosine], axis=1), jnp.concatenate([-sine, sine], axis=1)


def rotate(values, cosine, sine):
    return values * cosine + pltpu.roll(values, values.shape[-1] // 2, 1) * sine


class Place:
    def __init__(self, across, depth_count):
        self.chips, self.depth = across // 2, depth_count
        self.count = self.chips * depth_count
        member = lax.axis_index("gx")
        self.chip, self.core = member // 2, member % 2
        self.z = lax.axis_index("gz")

    def ahead(self, offset):
        return (
            lax.rem(self.chip + offset // self.depth, self.chips),
            lax.rem(self.z + offset % self.depth, self.depth),
        )

    def behind(self, offset):
        return (
            lax.rem(self.chip + self.chips - offset // self.depth, self.chips),
            lax.rem(self.z + self.depth - offset % self.depth, self.depth),
        )

    def device(self, chip, z, core):
        return {"gx": chip * 2 + core, "gz": z}

    def partner(self):
        return self.device(self.chip, self.z, 1 - self.core)

    def meet(self):
        barrier = pltpu.get_barrier_semaphore()
        pl.semaphore_signal(barrier, inc=1, device_id=self.partner(), device_id_type=MESH)
        for offset in range(1, self.count):
            chip, z = self.ahead(offset)
            pl.semaphore_signal(
                barrier, inc=1, device_id=self.device(chip, z, self.core), device_id_type=MESH
            )
        pl.semaphore_wait(barrier, self.count)


def send(src, dst, send_sem, recv_sem, device):
    return pltpu.make_async_remote_copy(
        src_ref=src,
        dst_ref=dst,
        send_sem=send_sem,
        recv_sem=recv_sem,
        device_id=device,
        device_id_type=MESH,
    )


def project_sum_kernel(
    x_ref, y_ref, wq_ref, wk_ref, wv_ref, wo_ref, q_out, g_out, kv_out,
    kv_give, kv_take, kv_mine, kv_land, kv_half, kv_other,
    q_give, q_take, q_mine, q_land,
    g_give, g_take, g_mine, g_land,
    pair_send, pair_recv, chip_send, chip_recv, half_send, half_recv,
    *, across, depth_count, sharers,
):
    at = Place(across, depth_count)
    block, columns = q_out.shape
    half = block // 2
    dtype = q_out.dtype
    tile = min(256, half)
    at.meet()
    give, take = (kv_give, q_give, g_give), (kv_take, q_take, g_take)
    mine, land = (kv_mine, q_mine, g_mine), (kv_land, q_land, g_land)

    def compute(which, offset):
        chip, z = at.ahead(offset)

        def rows(start, i):
            return pl.ds(pl.multiple_of(start + i * tile, tile), tile)

        def body(i, carry):
            here = pl.ds(pl.multiple_of(i * tile, tile), tile)
            for core, into in ((1 - at.core, give[which]), (at.core, mine[which])):
                if which == 0:
                    head = (2 * chip) // sharers
                    cols = pl.ds(pl.multiple_of(head * HD, HD), HD)
                    x = x_ref[rows(z * block + core * half, i), :]
                    into[offset, here, :HD] = dot(x, wk_ref[:, cols], 1, 0).astype(dtype)
                    into[offset, here, HD:] = dot(x, wv_ref[:, cols], 1, 0).astype(dtype)
                else:
                    cols = pl.ds(pl.multiple_of((chip * 2 + core) * columns, HD), columns)
                    if which == 1:
                        term = dot(x_ref[rows(z * block, i), :], wq_ref[:, cols], 1, 0)
                    else:
                        term = dot(y_ref[rows(z * block, i), :], wo_ref[cols, :], 1, 1)
                    into[offset, here, :] = term.astype(dtype)
            return carry

        lax.fori_loop(0, mine[which].shape[1] // tile, body, 0)
        copy = send(
            give[which].at[offset],
            take[which].at[offset],
            pair_send.at[which, offset],
            pair_recv.at[which, offset],
            at.partner(),
        )
        copy.start()
        return copy

    def forward(which, offset, pair_copy):
        pair_copy.wait_recv()

        def body(i, carry):
            here = pl.ds(pl.multiple_of(i * tile, tile), tile)
            total = mine[which][offset, here, :].astype(jnp.float32) + take[which][
                offset, here, :
            ].astype(jnp.float32)
            mine[which][offset, here, :] = total.astype(dtype)
            return carry

        lax.fori_loop(0, mine[which].shape[1] // tile, body, 0)
        if offset == 0:
            return None
        chip, z = at.ahead(offset)
        copy = send(
            mine[which].at[offset],
            land[which].at[offset - 1],
            chip_send.at[which, offset],
            chip_recv.at[which, offset],
            at.device(chip, z, at.core),
        )
        copy.start()
        return copy

    def finish(which, out):
        def body(i, carry):
            here = pl.ds(pl.multiple_of(i * tile, tile), tile)
            total = mine[which][0, here, :].astype(jnp.float32)
            for other in range(at.count - 1):
                total = total + land[which][other, here, :].astype(jnp.float32)
            out[here, :] = total.astype(dtype)
            return carry

        lax.fori_loop(0, mine[which].shape[1] // tile, body, 0)

    offsets = list(range(1, at.count)) + [0]
    steps = [(which, offset) for which in range(3) for offset in offsets]
    pairs, chips = [], [[], [], []]
    for which, offset in steps:
        pairs.append(compute(which, offset))
        done = len(pairs) - 2
        if done >= 0:
            before, place = steps[done]
            chips[before].append(forward(before, place, pairs[done]))
    chips[2].append(forward(2, 0, pairs[-1]))

    for copy in chips[0][:-1]:
        copy.wait_recv()
    finish(0, kv_half)
    swap = send(kv_half, kv_other, half_send, half_recv, at.partner())
    swap.start()
    for copy in chips[1][:-1]:
        copy.wait_recv()
    finish(1, q_out)
    swap.wait()
    kv_out[pl.ds(pl.multiple_of(at.core * half, half), half), :] = kv_half[...]
    kv_out[pl.ds(pl.multiple_of((1 - at.core) * half, half), half), :] = kv_other[...]
    for copy in chips[2][:-1]:
        copy.wait_recv()
    finish(2, g_out)
    for copy in pairs:
        copy.wait_send()
    for group in chips:
        for copy in group[:-1]:
            copy.wait_send()


def project_sum(x, y, wq, wk, wv, wo, across, depth_count, sharers):
    tokens = x.shape[0]
    block, columns = tokens // depth_count, wq.shape[1] // across
    half, count = block // 2, across // 2 * depth_count
    low = jnp.bfloat16

    def slots(number, rows, width):
        return pltpu.VMEM((number, rows, width), low)

    def buffers(rows, width):
        return [slots(count, rows, width)] * 3 + [slots(count - 1, rows, width)]

    dma = pltpu.SemaphoreType.DMA
    return pl.pallas_call(
        functools.partial(
            project_sum_kernel, across=across, depth_count=depth_count, sharers=sharers
        ),
        out_shape=(
            jax.ShapeDtypeStruct((block, columns), low),
            jax.ShapeDtypeStruct((block, columns), low),
            jax.ShapeDtypeStruct((block, 2 * HD), low),
        ),
        in_specs=[pl.BlockSpec(memory_space=pltpu.VMEM)] * 6,
        out_specs=(pl.BlockSpec(memory_space=pltpu.VMEM),) * 3,
        scratch_shapes=buffers(half, 2 * HD)
        + [pltpu.VMEM((half, 2 * HD), low)] * 2
        + buffers(block, columns)
        + buffers(block, columns)
        + [dma((3, count))] * 4
        + [dma, dma],
        compiler_params=pltpu.CompilerParams(
            vmem_limit_bytes=60 * 1024 * 1024, collective_id=0, has_side_effects=True
        ),
        cost_estimate=cost(4 * tokens * x.shape[1] * columns * across, 2**25),
    )(x, y, wq, wk, wv, wo)


def gather_kernel(*refs, number, across, depth_count):
    ins, outs = refs[:number], refs[number : 2 * number]
    chip_send, chip_recv, pair_send, pair_recv, own_sem = refs[2 * number :]
    at = Place(across, depth_count)
    member = at.chip * 2 + at.core
    at.meet()
    sends, chips, pairs, owns = [], {}, [], []
    for i in range(number):
        for offset in range(1, at.count):
            chip, z = at.ahead(offset)
            copy = send(
                ins[i],
                outs[i].at[member, at.z],
                chip_send.at[i, offset],
                chip_recv.at[i, offset],
                at.device(chip, z, at.core),
            )
            copy.start()
            sends.append(copy)
        copy = send(
            ins[i],
            outs[i].at[member, at.z],
            pair_send.at[i, 0],
            pair_recv.at[i, 0],
            at.partner(),
        )
        copy.start()
        pairs.append((i, 0, copy))
        own = pltpu.make_async_copy(ins[i], outs[i].at[member, at.z], own_sem.at[i])
        own.start()
        owns.append(own)
    for i in range(number):
        for offset in range(1, at.count):
            chip, z = at.behind(offset)
            arrived = outs[i].at[chip * 2 + at.core, z]
            send(
                ins[i],
                arrived,
                chip_send.at[i, offset],
                chip_recv.at[i, offset],
                at.device(chip, z, at.core),
            ).wait_recv()
            copy = send(
                arrived, arrived, pair_send.at[i, offset], pair_recv.at[i, offset], at.partner()
            )
            copy.start()
            pairs.append((i, offset, copy))
    for own in owns:
        own.wait()
    for copy in sends:
        copy.wait_send()
    for i, offset, copy in pairs:
        copy.wait_send()
        chip, z = at.behind(offset)
        send(
            ins[i],
            outs[i].at[chip * 2 + 1 - at.core, z],
            pair_send.at[i, offset],
            pair_recv.at[i, offset],
            at.partner(),
        ).wait_recv()


def gather(arrays, across, depth_count, collective_id):
    number, count = len(arrays), across // 2 * depth_count
    dma = pltpu.SemaphoreType.DMA
    return pl.pallas_call(
        functools.partial(gather_kernel, number=number, across=across, depth_count=depth_count),
        out_shape=tuple(
            jax.ShapeDtypeStruct((across, depth_count) + x.shape, x.dtype) for x in arrays
        ),
        in_specs=[pl.BlockSpec(memory_space=pl.ANY)] * number,
        out_specs=(pl.BlockSpec(memory_space=pl.ANY),) * number,
        scratch_shapes=[dma((number, count))] * 4 + [dma((number,))],
        compiler_params=pltpu.CompilerParams(
            vmem_limit_bytes=VMEM_LIMIT, collective_id=collective_id, has_side_effects=True
        ),
        cost_estimate=cost(0, 2**27),
    )(*arrays)


def attend_kernel(
    q_ref, g_ref, kv_ref, cos_ref, sin_ref, seg_col, seg_row, o_ref, dq_ref, dkv_ref, dk_acc, dv_acc, kr_ref, *, tile
):
    head = pl.program_id(0)
    rows = q_ref.shape[0]
    scale = 1.0 / math.sqrt(HD)

    @pl.when(head == 0)
    def _():
        dk_acc[...] = jnp.zeros_like(dk_acc)
        dv_acc[...] = jnp.zeros_like(dv_acc)
        keys = kv_ref[:, :HD].astype(jnp.float32)
        kr_ref[...] = rotate(keys, cos_ref[...], sin_ref[...]).astype(kr_ref.dtype)

    for step in range(rows // tile):
        here = pl.ds(step * tile, tile)
        width = (step + 1) * tile
        cosine, sine = cos_ref[here, :], sin_ref[here, :]
        query = rotate(q_ref[here, :].astype(jnp.float32), cosine, sine).astype(jnp.bfloat16)
        grad = g_ref[here, :].astype(jnp.bfloat16)
        keys = kr_ref[:width, :]
        values = kv_ref[:width, HD:]
        scores = dot(query, keys, 1, 1) * scale
        at_row = lax.broadcasted_iota(jnp.int32, scores.shape, 0) + step * tile
        at_col = lax.broadcasted_iota(jnp.int32, scores.shape, 1)
        allowed = (seg_col[here, :] == seg_row[:, :width]) & (at_col <= at_row)
        scores = jnp.where(allowed, scores, masked_score)
        weights = jnp.exp(scores - jnp.max(scores, axis=-1, keepdims=True))
        probs = weights * (1.0 / jnp.sum(weights, axis=-1, keepdims=True))
        probs_low = probs.astype(jnp.bfloat16)
        outputs = dot(probs_low, values, 1, 0).astype(jnp.bfloat16)
        o_ref[here, :] = outputs
        delta = jnp.sum(
            grad.astype(jnp.float32) * outputs.astype(jnp.float32), axis=-1, keepdims=True
        )
        dscore = (probs * (dot(grad, values, 1, 1) - delta)).astype(jnp.bfloat16)
        dquery = dot(dscore, keys, 1, 0) * scale
        dq_ref[here, :] = rotate(dquery, cosine, -sine).astype(dq_ref.dtype)
        dk_acc[:width, :] += dot(dscore, query, 0, 0) * scale
        dv_acc[:width, :] += dot(probs_low, grad, 0, 0)

    @pl.when(head == pl.num_programs(0) - 1)
    def _():
        dkv_ref[:, :HD] = rotate(dk_acc[...], cos_ref[...], -sin_ref[...]).astype(dkv_ref.dtype)
        dkv_ref[:, HD:] = dv_acc[...].astype(dkv_ref.dtype)


def attend(query, grad, kv, cosine, sine, segments):
    rows, columns = query.shape
    heads = columns // HD
    head_spec = pl.BlockSpec((rows, HD), lambda h: (0, h))

    def whole(shape):
        return pl.BlockSpec(shape, lambda h: (0, 0))

    return pl.pallas_call(
        functools.partial(attend_kernel, tile=min(256, rows)),
        grid=(heads,),
        out_shape=(
            jax.ShapeDtypeStruct((rows, columns), jnp.bfloat16),
            jax.ShapeDtypeStruct((rows, columns), jnp.bfloat16),
            jax.ShapeDtypeStruct((rows, 2 * HD), jnp.bfloat16),
        ),
        in_specs=[
            head_spec,
            head_spec,
            whole((rows, 2 * HD)),
            whole((rows, HD)),
            whole((rows, HD)),
            whole((rows, 1)),
            whole((1, rows)),
        ],
        out_specs=(head_spec, head_spec, whole((rows, 2 * HD))),
        scratch_shapes=[
            pltpu.VMEM((rows, HD), jnp.float32),
            pltpu.VMEM((rows, HD), jnp.float32),
            pltpu.VMEM((rows, HD), jnp.bfloat16),
        ],
        compiler_params=params(),
        cost_estimate=cost(10 * rows * rows * columns, 8 * 2**20),
    )(query, grad, kv, cosine, sine, segments[:, None], segments[None, :])


def input_grad_kernel(dq_ref, dkv_ref, wq_ref, wk_ref, wv_ref, o_ref):
    across, _, columns = dq_ref.shape
    total = None
    for m in range(across):
        term = dot(dq_ref[m], wq_ref[:, m * columns : (m + 1) * columns], 1, 1)
        total = term if total is None else total + term
    for g in range(dkv_ref.shape[0]):
        both = dkv_ref[g]
        total = total + dot(both[:, :HD], wk_ref[:, g * HD : (g + 1) * HD], 1, 1)
        total = total + dot(both[:, HD:], wv_ref[:, g * HD : (g + 1) * HD], 1, 1)
    o_ref[...] = total.astype(o_ref.dtype)


def input_grad_part(dq, dkv, wq, wk, wv):
    across, tokens, columns = dq.shape
    groups = dkv.shape[0]
    breadth = wq.shape[0]
    tile = min(256, tokens)

    def whole(x):
        return pl.BlockSpec(x.shape, lambda t: (0, 0))

    return pl.pallas_call(
        input_grad_kernel,
        grid=(tokens // tile,),
        out_shape=jax.ShapeDtypeStruct((tokens, breadth), jnp.bfloat16),
        in_specs=[
            pl.BlockSpec((across, tile, columns), lambda t: (0, t, 0)),
            pl.BlockSpec((groups, tile, 2 * HD), lambda t: (0, t, 0)),
            whole(wq),
            whole(wk),
            whole(wv),
        ],
        out_specs=pl.BlockSpec((tile, breadth), lambda t: (t, 0)),
        compiler_params=params(),
        cost_estimate=cost(2 * tokens * breadth * (columns * across + 2 * HD * groups), 2**24),
    )(dq, dkv, wq, wk, wv)


def qkv_grad_kernel(x_ref, dq_ref, dkv_ref, q_out, k_out, v_out, xt_ref):
    m = pl.program_id(0)

    @pl.when(m == 0)
    def _():
        xt_ref[...] = x_ref[...].T
        for g in range(dkv_ref.shape[0]):
            both = dot(xt_ref[...], dkv_ref[g], 1, 0).astype(k_out.dtype)
            k_out[:, g * HD : (g + 1) * HD] = both[:, :HD]
            v_out[:, g * HD : (g + 1) * HD] = both[:, HD:]

    q_out[...] = dot(xt_ref[...], dq_ref[0], 1, 0).astype(q_out.dtype)


def qkv_grads(x, dq, dkv):
    across, tokens, columns = dq.shape
    groups = dkv.shape[0]
    breadth = x.shape[1]
    return pl.pallas_call(
        qkv_grad_kernel,
        grid=(across,),
        out_shape=(
            jax.ShapeDtypeStruct((breadth, across * columns), jnp.bfloat16),
            jax.ShapeDtypeStruct((breadth, groups * HD), jnp.bfloat16),
            jax.ShapeDtypeStruct((breadth, groups * HD), jnp.bfloat16),
        ),
        in_specs=[
            pl.BlockSpec(x.shape, lambda m: (0, 0)),
            pl.BlockSpec((1, tokens, columns), lambda m: (m, 0, 0)),
            pl.BlockSpec(dkv.shape, lambda m: (0, 0, 0)),
        ],
        out_specs=(
            pl.BlockSpec((breadth, columns), lambda m: (0, m)),
            pl.BlockSpec((breadth, groups * HD), lambda m: (0, 0)),
            pl.BlockSpec((breadth, groups * HD), lambda m: (0, 0)),
        ),
        scratch_shapes=[pltpu.VMEM((breadth, tokens), jnp.bfloat16)],
        compiler_params=params(),
        cost_estimate=cost(2 * tokens * breadth * (columns * across + 2 * HD * groups), 2**24),
    )(x, dq, dkv)


def out_grad_kernel(a_ref, g_ref, o_ref):
    o_ref[...] = dot(a_ref[0].T, g_ref[...], 1, 0).astype(o_ref.dtype)


def out_grad(outputs, grad_out):
    across, tokens, columns = outputs.shape
    breadth = grad_out.shape[1]
    return pl.pallas_call(
        out_grad_kernel,
        grid=(across,),
        out_shape=jax.ShapeDtypeStruct((across * columns, breadth), jnp.bfloat16),
        in_specs=[
            pl.BlockSpec((1, tokens, columns), lambda m: (m, 0, 0)),
            pl.BlockSpec(grad_out.shape, lambda m: (0, 0)),
        ],
        out_specs=pl.BlockSpec((columns, breadth), lambda m: (m, 0)),
        compiler_params=params(),
        cost_estimate=cost(2 * tokens * breadth * columns * across, 2**24),
    )(outputs, grad_out)


def per_device(
    hidden_states,
    grad_out,
    query_weight,
    key_weight,
    value_weight,
    output_weight,
    segment_ids,
    positions,
):
    across = lax.axis_size("gx")
    depth_count = lax.axis_size("gz")
    token_count = hidden_states.shape[0]
    kv_groups = key_weight.shape[1] // HD
    sharers = across // kv_groups
    columns = query_weight.shape[1] // across

    query, grad_heads, kv = project_sum(
        hidden_states,
        grad_out,
        query_weight,
        key_weight,
        value_weight,
        output_weight,
        across,
        depth_count,
        sharers,
    )
    cosine, sine = rope_tables(positions, HD)
    outputs, dquery, dkv = attend(query, grad_heads, kv, cosine, sine, segment_ids)

    dkv_all, dq_all = gather((dkv, dquery), across, depth_count, 1)
    dkv_all = (
        dkv_all.reshape(kv_groups, sharers, token_count, 2 * HD)
        .astype(jnp.float32)
        .sum(axis=1)
        .astype(jnp.bfloat16)
    )
    dq_all = dq_all.reshape(across, token_count, columns)
    summed = input_grad_part(dq_all, dkv_all, query_weight, key_weight, value_weight)
    outputs, summed = lax.optimization_barrier((outputs, summed))
    input_grad = lax.psum_scatter(summed, "gy", scatter_dimension=0, tiled=True)
    (outputs_all,) = gather((outputs,), across, depth_count, 2)
    outputs_all = outputs_all.reshape(across, token_count, columns)
    query_weight_grad, key_weight_grad, value_weight_grad = qkv_grads(
        hidden_states, dq_all, dkv_all
    )
    output_weight_grad = out_grad(outputs_all, grad_out)
    return (input_grad, query_weight_grad, key_weight_grad, value_weight_grad, output_weight_grad)


def solution(mesh):
    placed = (
        P(None, GROUP),
        P(None, GROUP),
        P(GROUP, "gy"),
        P(GROUP, "gy"),
        P(GROUP, "gy"),
        P("gy", GROUP),
        P("gz"),
        P("gz"),
    )
    return jax.shard_map(
        per_device,
        mesh=mesh,
        in_specs=placed,
        out_specs=(
            P("gy", GROUP),
            P(GROUP, "gy"),
            P(GROUP, "gy"),
            P(GROUP, "gy"),
            P("gy", GROUP),
        ),
        check_vma=False,
    )
```

```python
import functools
import math

import jax
import jax.numpy as jnp
from jax import lax
from jax.experimental import pallas as pl
from jax.experimental.pallas import tpu as pltpu
from jax.sharding import PartitionSpec as P

HD = 128
GROUP = ("gx", "gz")
MESH = pl.DeviceIdType.MESH

rope_base = 10000.0
masked_score = -1e30
VMEM_LIMIT = 56 * 1024 * 1024


def params():
    return pltpu.CompilerParams(vmem_limit_bytes=VMEM_LIMIT)


def cost(flops, moved):
    return pl.CostEstimate(flops=flops, bytes_accessed=moved, transcendentals=0)


def dot(a, b, ca, cb):
    return lax.dot_general(a, b, (((ca,), (cb,)), ((), ())), preferred_element_type=jnp.float32)


def rope_tables(positions, head_size):
    halves = jnp.arange(head_size // 2, dtype=jnp.float32)
    inverse = rope_base ** (-2.0 * halves / head_size)
    angles = positions.astype(jnp.float32)[:, None] * inverse[None, :]
    cosine, sine = jnp.cos(angles), jnp.sin(angles)
    return jnp.concatenate([cosine, cosine], axis=1), jnp.concatenate([-sine, sine], axis=1)


def rotate(values, cosine, sine):
    return values * cosine + pltpu.roll(values, values.shape[-1] // 2, 1) * sine


class Place:
    def __init__(self, across, depth_count):
        self.chips, self.depth = across // 2, depth_count
        self.count = self.chips * depth_count
        self.square = self.chips == 2 and depth_count == 2
        member = lax.axis_index("gx")
        self.chip, self.core = member // 2, member % 2
        self.z = lax.axis_index("gz")

    def ahead(self, offset):
        return (
            lax.rem(self.chip + offset // self.depth, self.chips),
            lax.rem(self.z + offset % self.depth, self.depth),
        )

    def behind(self, offset):
        return (
            lax.rem(self.chip + self.chips - offset // self.depth, self.chips),
            lax.rem(self.z + self.depth - offset % self.depth, self.depth),
        )

    def device(self, chip, z, core):
        return {"gx": chip * 2 + core, "gz": z}

    def partner(self):
        return self.device(self.chip, self.z, 1 - self.core)

    def meet(self):
        barrier = pltpu.get_barrier_semaphore()
        pl.semaphore_signal(barrier, inc=1, device_id=self.partner(), device_id_type=MESH)
        for offset in range(1, self.count):
            chip, z = self.ahead(offset)
            pl.semaphore_signal(
                barrier, inc=1, device_id=self.device(chip, z, self.core), device_id_type=MESH
            )
        pl.semaphore_wait(barrier, self.count)


def send(src, dst, send_sem, recv_sem, device):
    return pltpu.make_async_remote_copy(
        src_ref=src,
        dst_ref=dst,
        send_sem=send_sem,
        recv_sem=recv_sem,
        device_id=device,
        device_id_type=MESH,
    )


def project_sum_kernel(
    x_ref, y_ref, wq_ref, wk_ref, wv_ref, wo_ref, q_out, g_out, kv_out,
    kv_give, kv_take, kv_mine, kv_land, kv_half, kv_other,
    q_give, q_take, q_mine, q_land,
    g_give, g_take, g_mine, g_land,
    pair_send, pair_recv, chip_send, chip_recv, half_send, half_recv, via_send, via_recv,
    *, across, depth_count, sharers,
):
    at = Place(across, depth_count)
    block, columns = q_out.shape
    half = block // 2
    dtype = q_out.dtype
    tile = min(256, half)
    at.meet()
    give, take = (kv_give, q_give, g_give), (kv_take, q_take, g_take)
    mine, land = (kv_mine, q_mine, g_mine), (kv_land, q_land, g_land)

    def compute(which, offset):
        chip, z = at.ahead(offset)

        def rows(start, i):
            return pl.ds(pl.multiple_of(start + i * tile, tile), tile)

        def body(i, carry):
            here = pl.ds(pl.multiple_of(i * tile, tile), tile)
            for core, into in ((1 - at.core, give[which]), (at.core, mine[which])):
                if which == 0:
                    head = (2 * chip) // sharers
                    cols = pl.ds(pl.multiple_of(head * HD, HD), HD)
                    x = x_ref[rows(z * block + core * half, i), :]
                    into[offset, here, :HD] = dot(x, wk_ref[:, cols], 1, 0).astype(dtype)
                    into[offset, here, HD:] = dot(x, wv_ref[:, cols], 1, 0).astype(dtype)
                else:
                    cols = pl.ds(pl.multiple_of((chip * 2 + core) * columns, HD), columns)
                    if which == 1:
                        term = dot(x_ref[rows(z * block, i), :], wq_ref[:, cols], 1, 0)
                    else:
                        term = dot(y_ref[rows(z * block, i), :], wo_ref[cols, :], 1, 1)
                    into[offset, here, :] = term.astype(dtype)
            return carry

        lax.fori_loop(0, mine[which].shape[1] // tile, body, 0)
        copy = send(
            give[which].at[offset],
            take[which].at[offset],
            pair_send.at[which, offset],
            pair_recv.at[which, offset],
            at.partner(),
        )
        copy.start()
        return copy

    def add_rows(which, offset, source, slot, start, number):
        def body(i, carry):
            here = pl.ds(pl.multiple_of(start + i * step, step), step)
            total = mine[which][offset, here, :].astype(jnp.float32) + source[
                slot, here, :
            ].astype(jnp.float32)
            mine[which][offset, here, :] = total.astype(dtype)
            return carry

        step = min(tile, number)
        lax.fori_loop(0, number // step, body, 0)

    def to_chip(which, offset, rows, slot, send_sem, recv_sem, target):
        chip, z = at.ahead(target)
        copy = send(
            mine[which].at[offset, rows],
            land[which].at[slot, rows],
            send_sem,
            recv_sem,
            at.device(chip, z, at.core),
        )
        copy.start()
        return copy

    def forward(which, offset, pair_copy):
        pair_copy.wait_recv()
        rows = mine[which].shape[1]
        add_rows(which, offset, take[which], offset, 0, rows)
        if offset == 0:
            return
        if at.square and offset == 3:
            via[which] = [
                to_chip(
                    which, 3, pl.ds(0, rows // 2), 2,
                    chip_send.at[which, 3], chip_recv.at[which, 3], 1,
                ),
                to_chip(
                    which, 3, pl.ds(rows // 2, rows // 2), 2,
                    via_send.at[which], via_recv.at[which], 2,
                ),
            ]
            return
        if at.square:
            passed = 2 - offset
            via[which][passed].wait_recv()
            add_rows(which, offset, land[which], 2, passed * (rows // 2), rows // 2)
        direct[which].append(
            to_chip(
                which, offset, pl.ds(0, rows), offset - 1,
                chip_send.at[which, offset], chip_recv.at[which, offset], offset,
            )
        )

    def finish(which, out):
        def body(i, carry):
            here = pl.ds(pl.multiple_of(i * tile, tile), tile)
            total = mine[which][0, here, :].astype(jnp.float32)
            for other in range(2 if at.square else at.count - 1):
                total = total + land[which][other, here, :].astype(jnp.float32)
            out[here, :] = total.astype(dtype)
            return carry

        lax.fori_loop(0, mine[which].shape[1] // tile, body, 0)

    order = (1, 0, 2)
    if at.square:
        steps = [(1, 3), (2, 3), (0, 3)] + [(which, k) for which in order for k in (1, 2)]
    else:
        steps = [(which, k) for which in order for k in range(1, at.count)]
    steps = steps + [(which, 0) for which in order]
    pairs, via, direct = [], {}, ([], [], [])
    for which, offset in steps:
        pairs.append(compute(which, offset))
        done = len(pairs) - 2
        if done >= 0:
            forward(*steps[done], pairs[done])
    forward(*steps[-1], pairs[-1])

    for copy in direct[0]:
        copy.wait_recv()
    finish(0, kv_half)
    swap = send(kv_half, kv_other, half_send, half_recv, at.partner())
    swap.start()
    for copy in direct[1]:
        copy.wait_recv()
    finish(1, q_out)
    swap.wait()
    kv_out[pl.ds(pl.multiple_of(at.core * half, half), half), :] = kv_half[...]
    kv_out[pl.ds(pl.multiple_of((1 - at.core) * half, half), half), :] = kv_other[...]
    for copy in direct[2]:
        copy.wait_recv()
    finish(2, g_out)
    for copy in pairs:
        copy.wait_send()
    for which in range(3):
        for copy in direct[which] + via.get(which, []):
            copy.wait_send()


def project_sum(x, y, wq, wk, wv, wo, across, depth_count, sharers):
    tokens = x.shape[0]
    block, columns = tokens // depth_count, wq.shape[1] // across
    half, count = block // 2, across // 2 * depth_count
    low = jnp.bfloat16

    def slots(number, rows, width):
        return pltpu.VMEM((number, rows, width), low)

    def buffers(rows, width):
        return [slots(count, rows, width)] * 3 + [slots(count - 1, rows, width)]

    dma = pltpu.SemaphoreType.DMA
    return pl.pallas_call(
        functools.partial(
            project_sum_kernel, across=across, depth_count=depth_count, sharers=sharers
        ),
        out_shape=(
            jax.ShapeDtypeStruct((block, columns), low),
            jax.ShapeDtypeStruct((block, columns), low),
            jax.ShapeDtypeStruct((block, 2 * HD), low),
        ),
        in_specs=[pl.BlockSpec(memory_space=pltpu.VMEM)] * 6,
        out_specs=(pl.BlockSpec(memory_space=pltpu.VMEM),) * 3,
        scratch_shapes=buffers(half, 2 * HD)
        + [pltpu.VMEM((half, 2 * HD), low)] * 2
        + buffers(block, columns)
        + buffers(block, columns)
        + [dma((3, count))] * 4
        + [dma, dma, dma((3,)), dma((3,))],
        compiler_params=pltpu.CompilerParams(
            vmem_limit_bytes=60 * 1024 * 1024, collective_id=0, has_side_effects=True
        ),
        cost_estimate=cost(4 * tokens * x.shape[1] * columns * across, 2**25),
    )(x, y, wq, wk, wv, wo)


def gather_kernel(*refs, number, across, depth_count):
    ins, outs = refs[:number], refs[number : 2 * number]
    chip_send, chip_recv, pair_send, pair_recv, own_sem, via_send, via_recv = refs[2 * number :]
    at = Place(across, depth_count)
    member = at.chip * 2 + at.core
    at.meet()
    halves = [x.shape[0] // 2 for x in ins]
    sends, pairs, owns = [], [], []
    for i in range(number):
        for offset in range(1, 3 if at.square else at.count):
            chip, z = at.ahead(offset)
            copy = send(
                ins[i],
                outs[i].at[member, at.z],
                chip_send.at[i, offset],
                chip_recv.at[i, offset],
                at.device(chip, z, at.core),
            )
            copy.start()
            sends.append(copy)
        copy = send(
            ins[i],
            outs[i].at[member, at.z],
            pair_send.at[i, 0],
            pair_recv.at[i, 0],
            at.partner(),
        )
        copy.start()
        pairs.append((i, 0, copy))
        own = pltpu.make_async_copy(ins[i], outs[i].at[member, at.z], own_sem.at[i])
        own.start()
        owns.append(own)
    for i in range(number):
        for offset in range(1, at.count):
            chip, z = at.behind(offset)
            arrived = outs[i].at[chip * 2 + at.core, z]
            if at.square and offset == 3:
                for part, (send_sem, recv_sem) in enumerate(
                    (
                        (chip_send.at[i, 3], chip_recv.at[i, 3]),
                        (via_send.at[i], via_recv.at[i]),
                    )
                ):
                    piece = pl.ds(part * halves[i], halves[i])
                    send(
                        ins[i].at[piece],
                        arrived.at[piece],
                        send_sem,
                        recv_sem,
                        at.device(chip, z, at.core),
                    ).wait_recv()
            else:
                send(
                    ins[i],
                    arrived,
                    chip_send.at[i, offset],
                    chip_recv.at[i, offset],
                    at.device(chip, z, at.core),
                ).wait_recv()
                if at.square:
                    piece = pl.ds((offset - 1) * halves[i], halves[i])
                    next_chip, next_z = at.ahead(3 - offset)
                    sems = (chip_send.at[i, 3], chip_recv.at[i, 3])
                    if offset == 2:
                        sems = (via_send.at[i], via_recv.at[i])
                    copy = send(
                        arrived.at[piece],
                        arrived.at[piece],
                        *sems,
                        at.device(next_chip, next_z, at.core),
                    )
                    copy.start()
                    sends.append(copy)
            copy = send(
                arrived, arrived, pair_send.at[i, offset], pair_recv.at[i, offset], at.partner()
            )
            copy.start()
            pairs.append((i, offset, copy))
    for own in owns:
        own.wait()
    for copy in sends:
        copy.wait_send()
    for i, offset, copy in pairs:
        copy.wait_send()
        chip, z = at.behind(offset)
        send(
            ins[i],
            outs[i].at[chip * 2 + 1 - at.core, z],
            pair_send.at[i, offset],
            pair_recv.at[i, offset],
            at.partner(),
        ).wait_recv()


def gather(arrays, across, depth_count, collective_id):
    number, count = len(arrays), across // 2 * depth_count
    dma = pltpu.SemaphoreType.DMA
    return pl.pallas_call(
        functools.partial(gather_kernel, number=number, across=across, depth_count=depth_count),
        out_shape=tuple(
            jax.ShapeDtypeStruct((across, depth_count) + x.shape, x.dtype) for x in arrays
        ),
        in_specs=[pl.BlockSpec(memory_space=pl.ANY)] * number,
        out_specs=(pl.BlockSpec(memory_space=pl.ANY),) * number,
        scratch_shapes=[dma((number, count))] * 4 + [dma((number,))] * 3,
        compiler_params=pltpu.CompilerParams(
            vmem_limit_bytes=VMEM_LIMIT, collective_id=collective_id, has_side_effects=True
        ),
        cost_estimate=cost(0, 2**27),
    )(*arrays)


def attend_kernel(
    q_ref, g_ref, kv_ref, cos_ref, sin_ref, seg_col, seg_row, o_ref, dq_ref, dkv_ref, dk_acc, dv_acc, kr_ref, *, tile
):
    head = pl.program_id(0)
    rows = q_ref.shape[0]
    scale = 1.0 / math.sqrt(HD)

    @pl.when(head == 0)
    def _():
        dk_acc[...] = jnp.zeros_like(dk_acc)
        dv_acc[...] = jnp.zeros_like(dv_acc)
        keys = kv_ref[:, :HD].astype(jnp.float32)
        kr_ref[...] = rotate(keys, cos_ref[...], sin_ref[...]).astype(kr_ref.dtype)

    for step in range(rows // tile):
        here = pl.ds(step * tile, tile)
        width = (step + 1) * tile
        cosine, sine = cos_ref[here, :], sin_ref[here, :]
        query = rotate(q_ref[here, :].astype(jnp.float32), cosine, sine).astype(jnp.bfloat16)
        grad = g_ref[here, :].astype(jnp.bfloat16)
        keys = kr_ref[:width, :]
        values = kv_ref[:width, HD:]
        scores = dot(query, keys, 1, 1) * scale
        at_row = lax.broadcasted_iota(jnp.int32, scores.shape, 0) + step * tile
        at_col = lax.broadcasted_iota(jnp.int32, scores.shape, 1)
        allowed = (seg_col[here, :] == seg_row[:, :width]) & (at_col <= at_row)
        scores = jnp.where(allowed, scores, masked_score)
        weights = jnp.exp(scores - jnp.max(scores, axis=-1, keepdims=True))
        probs = weights * (1.0 / jnp.sum(weights, axis=-1, keepdims=True))
        probs_low = probs.astype(jnp.bfloat16)
        outputs = dot(probs_low, values, 1, 0).astype(jnp.bfloat16)
        o_ref[here, :] = outputs
        delta = jnp.sum(
            grad.astype(jnp.float32) * outputs.astype(jnp.float32), axis=-1, keepdims=True
        )
        dscore = (probs * (dot(grad, values, 1, 1) - delta)).astype(jnp.bfloat16)
        dquery = dot(dscore, keys, 1, 0) * scale
        dq_ref[here, :] = rotate(dquery, cosine, -sine).astype(dq_ref.dtype)
        dk_acc[:width, :] += dot(dscore, query, 0, 0) * scale
        dv_acc[:width, :] += dot(probs_low, grad, 0, 0)

    @pl.when(head == pl.num_programs(0) - 1)
    def _():
        dkv_ref[:, :HD] = rotate(dk_acc[...], cos_ref[...], -sin_ref[...]).astype(dkv_ref.dtype)
        dkv_ref[:, HD:] = dv_acc[...].astype(dkv_ref.dtype)


def attend(query, grad, kv, cosine, sine, segments):
    rows, columns = query.shape
    heads = columns // HD
    head_spec = pl.BlockSpec((rows, HD), lambda h: (0, h))

    def whole(shape):
        return pl.BlockSpec(shape, lambda h: (0, 0))

    return pl.pallas_call(
        functools.partial(attend_kernel, tile=min(256, rows)),
        grid=(heads,),
        out_shape=(
            jax.ShapeDtypeStruct((rows, columns), jnp.bfloat16),
            jax.ShapeDtypeStruct((rows, columns), jnp.bfloat16),
            jax.ShapeDtypeStruct((rows, 2 * HD), jnp.bfloat16),
        ),
        in_specs=[
            head_spec,
            head_spec,
            whole((rows, 2 * HD)),
            whole((rows, HD)),
            whole((rows, HD)),
            whole((rows, 1)),
            whole((1, rows)),
        ],
        out_specs=(head_spec, head_spec, whole((rows, 2 * HD))),
        scratch_shapes=[
            pltpu.VMEM((rows, HD), jnp.float32),
            pltpu.VMEM((rows, HD), jnp.float32),
            pltpu.VMEM((rows, HD), jnp.bfloat16),
        ],
        compiler_params=params(),
        cost_estimate=cost(10 * rows * rows * columns, 8 * 2**20),
    )(query, grad, kv, cosine, sine, segments[:, None], segments[None, :])


def input_grad_kernel(dq_ref, dkv_ref, wq_ref, wk_ref, wv_ref, o_ref):
    across, _, columns = dq_ref.shape
    total = None
    for m in range(across):
        term = dot(dq_ref[m], wq_ref[:, m * columns : (m + 1) * columns], 1, 1)
        total = term if total is None else total + term
    for g in range(dkv_ref.shape[0]):
        both = dkv_ref[g]
        total = total + dot(both[:, :HD], wk_ref[:, g * HD : (g + 1) * HD], 1, 1)
        total = total + dot(both[:, HD:], wv_ref[:, g * HD : (g + 1) * HD], 1, 1)
    o_ref[...] = total.astype(o_ref.dtype)


def input_grad_part(dq, dkv, wq, wk, wv):
    across, tokens, columns = dq.shape
    groups = dkv.shape[0]
    breadth = wq.shape[0]
    tile = min(256, tokens)

    def whole(x):
        return pl.BlockSpec(x.shape, lambda t: (0, 0))

    return pl.pallas_call(
        input_grad_kernel,
        grid=(tokens // tile,),
        out_shape=jax.ShapeDtypeStruct((tokens, breadth), jnp.bfloat16),
        in_specs=[
            pl.BlockSpec((across, tile, columns), lambda t: (0, t, 0)),
            pl.BlockSpec((groups, tile, 2 * HD), lambda t: (0, t, 0)),
            whole(wq),
            whole(wk),
            whole(wv),
        ],
        out_specs=pl.BlockSpec((tile, breadth), lambda t: (t, 0)),
        compiler_params=params(),
        cost_estimate=cost(2 * tokens * breadth * (columns * across + 2 * HD * groups), 2**24),
    )(dq, dkv, wq, wk, wv)


def qkv_grad_kernel(x_ref, dq_ref, dkv_ref, q_out, k_out, v_out, xt_ref):
    m = pl.program_id(0)

    @pl.when(m == 0)
    def _():
        xt_ref[...] = x_ref[...].T
        for g in range(dkv_ref.shape[0]):
            both = dot(xt_ref[...], dkv_ref[g], 1, 0).astype(k_out.dtype)
            k_out[:, g * HD : (g + 1) * HD] = both[:, :HD]
            v_out[:, g * HD : (g + 1) * HD] = both[:, HD:]

    q_out[...] = dot(xt_ref[...], dq_ref[0], 1, 0).astype(q_out.dtype)


def qkv_grads(x, dq, dkv):
    across, tokens, columns = dq.shape
    groups = dkv.shape[0]
    breadth = x.shape[1]
    return pl.pallas_call(
        qkv_grad_kernel,
        grid=(across,),
        out_shape=(
            jax.ShapeDtypeStruct((breadth, across * columns), jnp.bfloat16),
            jax.ShapeDtypeStruct((breadth, groups * HD), jnp.bfloat16),
            jax.ShapeDtypeStruct((breadth, groups * HD), jnp.bfloat16),
        ),
        in_specs=[
            pl.BlockSpec(x.shape, lambda m: (0, 0)),
            pl.BlockSpec((1, tokens, columns), lambda m: (m, 0, 0)),
            pl.BlockSpec(dkv.shape, lambda m: (0, 0, 0)),
        ],
        out_specs=(
            pl.BlockSpec((breadth, columns), lambda m: (0, m)),
            pl.BlockSpec((breadth, groups * HD), lambda m: (0, 0)),
            pl.BlockSpec((breadth, groups * HD), lambda m: (0, 0)),
        ),
        scratch_shapes=[pltpu.VMEM((breadth, tokens), jnp.bfloat16)],
        compiler_params=params(),
        cost_estimate=cost(2 * tokens * breadth * (columns * across + 2 * HD * groups), 2**24),
    )(x, dq, dkv)


def out_grad_kernel(a_ref, g_ref, o_ref):
    o_ref[...] = dot(a_ref[0].T, g_ref[...], 1, 0).astype(o_ref.dtype)


def out_grad(outputs, grad_out):
    across, tokens, columns = outputs.shape
    breadth = grad_out.shape[1]
    return pl.pallas_call(
        out_grad_kernel,
        grid=(across,),
        out_shape=jax.ShapeDtypeStruct((across * columns, breadth), jnp.bfloat16),
        in_specs=[
            pl.BlockSpec((1, tokens, columns), lambda m: (m, 0, 0)),
            pl.BlockSpec(grad_out.shape, lambda m: (0, 0)),
        ],
        out_specs=pl.BlockSpec((columns, breadth), lambda m: (m, 0)),
        compiler_params=params(),
        cost_estimate=cost(2 * tokens * breadth * columns * across, 2**24),
    )(outputs, grad_out)


def per_device(
    hidden_states,
    grad_out,
    query_weight,
    key_weight,
    value_weight,
    output_weight,
    segment_ids,
    positions,
):
    across = lax.axis_size("gx")
    depth_count = lax.axis_size("gz")
    token_count = hidden_states.shape[0]
    kv_groups = key_weight.shape[1] // HD
    sharers = across // kv_groups
    columns = query_weight.shape[1] // across

    query, grad_heads, kv = project_sum(
        hidden_states,
        grad_out,
        query_weight,
        key_weight,
        value_weight,
        output_weight,
        across,
        depth_count,
        sharers,
    )
    cosine, sine = rope_tables(positions, HD)
    outputs, dquery, dkv = attend(query, grad_heads, kv, cosine, sine, segment_ids)

    dkv_all, dq_all = gather((dkv, dquery), across, depth_count, 1)
    dkv_all = (
        dkv_all.reshape(kv_groups, sharers, token_count, 2 * HD)
        .astype(jnp.float32)
        .sum(axis=1)
        .astype(jnp.bfloat16)
    )
    dq_all = dq_all.reshape(across, token_count, columns)
    summed = input_grad_part(dq_all, dkv_all, query_weight, key_weight, value_weight)
    outputs, summed = lax.optimization_barrier((outputs, summed))
    input_grad = lax.psum_scatter(summed, "gy", scatter_dimension=0, tiled=True)
    (outputs_all,) = gather((outputs,), across, depth_count, 2)
    outputs_all = outputs_all.reshape(across, token_count, columns)
    query_weight_grad, key_weight_grad, value_weight_grad = qkv_grads(
        hidden_states, dq_all, dkv_all
    )
    output_weight_grad = out_grad(outputs_all, grad_out)
    return (input_grad, query_weight_grad, key_weight_grad, value_weight_grad, output_weight_grad)


def solution(mesh):
    placed = (
        P(None, GROUP),
        P(None, GROUP),
        P(GROUP, "gy"),
        P(GROUP, "gy"),
        P(GROUP, "gy"),
        P("gy", GROUP),
        P("gz"),
        P("gz"),
    )
    return jax.shard_map(
        per_device,
        mesh=mesh,
        in_specs=placed,
        out_specs=(
            P("gy", GROUP),
            P(GROUP, "gy"),
            P(GROUP, "gy"),
            P(GROUP, "gy"),
            P("gy", GROUP),
        ),
        check_vma=False,
    )
```
